32 devices in a mesh: seq: 8 (over z, y), mp: 4 (over x, core).
Axes of the slice: x: 2, y: 2, z: 4, core: 2. Of those that a mesh axis runs over, the one named last changes fastest.
Arguments:
- queries: bfloat16 [3072, 2048], P('seq', 'mp'), may hold values from -110 to 110
- self_keys: bfloat16 [3072, 2048], P('seq', 'mp'), may hold values from -6 to 6
- self_values: bfloat16 [3072, 2048], P('seq', 'mp'), may hold values from -6 to 6
- cross_query: bfloat16 [3072, 2048], P('seq', 'mp'), may hold values from -110 to 110
- memory_keys: bfloat16 [64, 128, 2048], P('seq', None, 'mp'), may hold values from -6 to 6
- memory_values: bfloat16 [64, 128, 2048], P('seq', None, 'mp'), may hold values from -6 to 6
- neighbour_owner: int32 [48, 2], P('seq'), may hold values from 0 to 7, all different within a row; in each aligned block of 6 rows (0 to 5, 6 to 11, ...) at most 2 rows name the same one
- neighbour_slot: int32 [48, 2], P('seq'), may hold values from 0 to 7
- out_weight: bfloat16 [2048, 4096], P('mp'), may hold values from -0.125 to 0.125
- cross_weight: bfloat16 [2048, 4096], P('mp'), may hold values from -0.125 to 0.125
Outputs:
- block_out: bfloat16 [3072, 4096], P('seq', 'mp')
The draws below stay inside these ranges and needn't reach their ends.
Inputs may be any that keep to these rules, and one draw needn't show every extreme that they name: `neighbour_owner`: the 2 neighbours of a span have different owners; among the spans of one index of seq, at most 2 neighbours have one owner.
All inputs are finite; a program needn't handle non-finite values.
Results may differ from the reference program's by a relative error of at most 0.025.
Values may be sent and summed in bfloat16 or wider, within the bound.
A program may use at most 128 MiB of HBM per device.

```python
import math
import jax
import jax.numpy as jnp
import numpy as np
from jax import lax

D = 4096
HEADS = 16
HEAD = 128
SPAN = 64
NB_LEN = 128
NEIGH = 2
TOK_DEV = 384
NB_DEV = 8
HD_ALL = 2048
TOKENS = 3072
SPANS_DEV = 6
SPANS = 48
NEIGHBOURS = 64
CAP = 2
N_SEQ = 8
N_MP = 4


def base_field(key, salt, shape, scale):
    subkey = jax.random.fold_in(key, salt)
    return jnp.clip(jax.random.normal(subkey, shape, jnp.float32), -6.0, 6.0) * scale


def draw_queries(key, part):
    sample = base_field(key, 11, (TOKENS, HEADS * HEAD), 2.5)
    return sample.astype(jnp.bfloat16)


def draw_self_keys(key, part):
    sample = base_field(key, 12, (TOKENS, HEADS * HEAD), 1.0)
    return sample.astype(jnp.bfloat16)


def draw_cross_query(key, part):
    sample = base_field(key, 13, (TOKENS, HEADS * HEAD), 2.0)
    return sample.astype(jnp.bfloat16)


def draw_memory_keys(key, part):
    sample = base_field(key, 14, (NB_DEV * N_SEQ, NB_LEN, HEADS * HEAD), 1.0)
    return sample.astype(jnp.bfloat16)


def touch_ends(entries, stream_key, low, high):
    place = [jax.random.randint(jax.random.fold_in(stream_key, axis), (), 0, length) for axis, length in enumerate(entries.shape)]
    widest = entries.shape.index(max(entries.shape))
    beside = place[:widest] + [(place[widest] + 1) % entries.shape[widest]] + place[widest + 1:]
    return entries.at[tuple(place)].set(low).at[tuple(beside)].set(high)


def block_levels(stream_key, extent, shards, smallest, largest):
    level = 1.0
    for axis_at, blocks in shards:
        heights = jax.random.uniform(jax.random.fold_in(jax.random.fold_in(stream_key, 6), axis_at), (blocks,), jnp.float32, smallest / len(shards), largest / len(shards))
        level = level * jnp.repeat(jnp.exp(heights), extent[axis_at] // blocks).reshape((-1,) + (1,) * (len(extent) - 1 - axis_at))
    return level


def assign_block(key, own, number, rows, number_of, top, reach, slope):
    order = jax.random.permutation(key, number_of)
    packed, ordinary = load_shares(number_of, rows * top, reach, slope, True), load_shares(number_of, rows * top, reach, slope, False)
    places = jnp.arange(number_of)

    def named(tallies, rotation):
        used = int((tallies > 0).sum())
        fixed = max(1, used // 4)
        moved = fixed + (places - fixed + rotation * (used - fixed)) % max(1, number_of - fixed)
        return jnp.zeros((number_of,), jnp.int32).at[order[jnp.where(places < fixed, places, moved)]].set(jnp.asarray(tallies, jnp.int32))

    tallies = jnp.where(number % 4 == 0, named(packed, number // 4), named(ordinary, number - number // 4 - 1))
    mixed = jax.random.permutation(jax.random.fold_in(own, 3), number_of)
    giver, receiver = mixed[0:number_of // 2 * 2:2], mixed[1:number_of // 2 * 2:2]
    room = jnp.minimum(tallies[giver] - 1, reach - tallies[receiver]) // 2
    room = jnp.where((giver == order[0]) | (receiver == order[0]) | (tallies[receiver] == 0), 0, jnp.maximum(room, 0))
    moved = jax.random.randint(jax.random.fold_in(own, 4), (number_of // 2,), 0, 1 << 20) % (room + 1)
    tallies = tallies.at[giver].add(-moved).at[receiver].add(moved)
    items = jnp.searchsorted(jnp.cumsum(tallies), jnp.arange(rows * top), side="right").astype(jnp.int32)
    listing = items.reshape(top, rows).T
    listing = listing[jax.random.permutation(jax.random.fold_in(own, 1), rows)]
    rotation = jax.random.randint(jax.random.fold_in(own, 2), (rows, 1), 0, top)
    return jnp.take_along_axis(listing, (jnp.arange(top)[None, :] + rotation) % top, axis=1)


def load_shares(amount, total, bound, skew, full):
    loads = [(1 << 20) // math.isqrt(grade ** skew) + 1 for grade in range(1, amount + 1)]
    largest = bound if full else min(bound, max(-(-total // amount), total * loads[0] // sum(loads)))
    least = 1 if total - largest >= amount - 1 else 0
    holding, surplus = [largest] + [least] * (amount - 1), total - largest - least * (amount - 1)
    while surplus > 0:
        candidates = [i for i in range(1, amount) if holding[i] < largest] or [i for i in range(1, amount) if holding[i] < bound]
        whole, budget = sum([loads[i] for i in candidates]), surplus
        for i in candidates:
            addition = min(bound - holding[i], max(1, budget * loads[i] // whole), surplus)
            holding[i] = holding[i] + addition
            surplus = surplus - addition
    return np.array(holding)


def noise(stream_key, dims, width, reach, split=(), kind=jnp.bfloat16):
    level = block_levels(stream_key, dims, split, -0.22, 0.18) if split else 1.0
    values = jax.random.normal(stream_key, dims, jnp.float32) * width * level
    return jnp.minimum(jnp.maximum(values, -reach), reach).astype(kind)


def setup_inputs(seed: int = 0) -> dict:
    key_of = jax.random.split(jax.random.key(seed), 11)
    queries = draw_queries(jax.random.fold_in(key_of[10], 71), 0)
    self_keys = draw_self_keys(jax.random.fold_in(key_of[10], 71), 0)
    self_values = noise(key_of[2], (TOKENS, HD_ALL), 1.0, 6.0, ((0, 8), (1, 4)))
    cross_query = draw_cross_query(jax.random.fold_in(key_of[10], 71), 0)
    memory_keys = draw_memory_keys(jax.random.fold_in(key_of[10], 71), 0)
    memory_values = noise(key_of[5], (NEIGHBOURS, NB_LEN, HD_ALL), 1.0, 6.0, ((0, 8), (2, 4)))
    neighbour_owner_keys = jax.random.split(jax.random.fold_in(key_of[6], 1), SPANS // SPANS_DEV)
    neighbour_owner_turns = jax.random.permutation(jax.random.fold_in(key_of[6], 3), SPANS // SPANS_DEV)
    neighbour_owner = jax.vmap(lambda own, number: assign_block(jax.random.fold_in(key_of[6], 2), own, number, SPANS_DEV, N_SEQ, NEIGH, CAP, 2))(neighbour_owner_keys, neighbour_owner_turns).reshape((SPANS, NEIGH))
    neighbour_slot = touch_ends(jax.random.randint(key_of[7], (SPANS, NEIGH), 0, NB_DEV), jax.random.fold_in(key_of[7], 1), 0, NB_DEV - 1).astype(jnp.int32)
    out_weight = noise(key_of[8], (HD_ALL, D), HD_ALL ** -0.5, 0.125, ((0, 4),))
    cross_weight = noise(key_of[9], (HD_ALL, D), HD_ALL ** -0.5, 0.125, ((0, 4),))
    return {"queries": queries, "self_keys": self_keys, "self_values": self_values, "cross_query": cross_query, "memory_keys": memory_keys, "memory_values": memory_values, "neighbour_owner": neighbour_owner, "neighbour_slot": neighbour_slot, "out_weight": out_weight, "cross_weight": cross_weight}


NEG_FILL = -1.0e30


def reference(queries, self_keys, self_values, cross_query, memory_keys, memory_values, neighbour_owner, neighbour_slot, out_weight, cross_weight):
    scale = HEAD ** -0.5
    key_heads = self_keys.astype(jnp.float32).reshape(TOKENS, HEADS, HEAD)
    value_heads = self_values.astype(jnp.float32).reshape(TOKENS, HEADS, HEAD)
    query_blocks = queries.reshape(TOKENS // TOK_DEV, TOK_DEV, HEADS, HEAD)
    block_starts = jnp.arange(TOKENS // TOK_DEV, dtype=jnp.int32) * TOK_DEV
    positions = jnp.arange(TOKENS, dtype=jnp.int32)

    def self_block(inputs):
        query_block, first_row = inputs
        scores = jnp.einsum("tha,uha->htu", query_block.astype(jnp.float32), key_heads, precision=lax.Precision.HIGHEST) * scale
        row_ids = first_row + jnp.arange(TOK_DEV, dtype=jnp.int32)
        allowed = row_ids[:, None] >= positions[None, :]
        masked = jnp.where(allowed[None], scores, NEG_FILL)
        highest = jnp.max(masked, axis=2)
        weights = jnp.exp(masked - highest[..., None])
        totals = jnp.sum(weights, axis=2)
        rounded = lax.optimization_barrier(weights.astype(jnp.bfloat16)).astype(jnp.float32)
        blended = jnp.einsum("htu,uha->tha", rounded, value_heads, precision=lax.Precision.HIGHEST)
        return (blended / jnp.transpose(totals)[..., None]).astype(jnp.bfloat16)

    attended = lax.map(self_block, (query_blocks, block_starts)).reshape(TOKENS, HD_ALL)

    tile_index = (neighbour_owner * NB_DEV + neighbour_slot).astype(jnp.int32)
    cross_blocks = cross_query.reshape(SPANS, SPAN, HEADS, HEAD)

    def cross_span(inputs):
        query_span, tiles = inputs
        key_tiles = memory_keys[tiles].astype(jnp.float32).reshape(NEIGH, NB_LEN, HEADS, HEAD)
        value_tiles = memory_values[tiles].astype(jnp.float32).reshape(NEIGH, NB_LEN, HEADS, HEAD)
        scores = jnp.einsum("cha,nkha->nhck", query_span.astype(jnp.float32), key_tiles, precision=lax.Precision.HIGHEST) * scale
        highest = jnp.max(scores, axis=3)
        weights = jnp.exp(scores - highest[..., None])
        totals = jnp.sum(weights, axis=3)
        rounded = lax.optimization_barrier(weights.astype(jnp.bfloat16)).astype(jnp.float32)
        blended = jnp.einsum("nhck,nkha->ncha", rounded, value_tiles, precision=lax.Precision.HIGHEST)
        blended = blended / jnp.transpose(totals, (0, 2, 1))[..., None]
        answer = lax.optimization_barrier(blended.astype(jnp.bfloat16)).astype(jnp.float32)
        log_mass = highest + jnp.log(totals)
        best_mass = jnp.max(log_mass, axis=0, keepdims=True)
        shares = jnp.exp(log_mass - best_mass)
        share_cols = jnp.transpose(shares, (0, 2, 1))[..., None]
        combined = jnp.sum(share_cols * answer, axis=0) / jnp.sum(share_cols, axis=0)
        return combined.astype(jnp.bfloat16)

    retrieved = lax.map(cross_span, (cross_blocks, tile_index)).reshape(TOKENS, HD_ALL)

    group_width = HD_ALL // N_MP
    summed = jnp.zeros((TOKENS, D), jnp.float32)
    for group_index in range(N_MP):
        first_col = group_index * group_width
        term = jnp.dot(attended[:, first_col:first_col + group_width], out_weight[first_col:first_col + group_width], preferred_element_type=jnp.float32)
        term = term + jnp.dot(retrieved[:, first_col:first_col + group_width], cross_weight[first_col:first_col + group_width], preferred_element_type=jnp.float32)
        summed = summed + lax.optimization_barrier(term.astype(jnp.bfloat16)).astype(jnp.float32)
    return summed.astype(jnp.bfloat16)
```

```python
import functools
import math

import jax
import jax.numpy as jnp
from jax import lax
from jax.experimental import pallas as pl
from jax.experimental.pallas import tpu as pltpu
from jax.sharding import PartitionSpec as P

HEAD = 128
SPAN = 64
NEG_FILL = -1e30
SCALE = HEAD ** (-0.5)
LOG2E = math.log2(math.e)
INFO = 16
F32 = jnp.float32
BF16 = jnp.bfloat16


def pack_heads_kernel(q_ref, k_ref, v_ref, out_ref):
    piece = q_ref.shape[0]
    rows = k_ref.shape[0]
    out_ref[0, :piece] = q_ref[...]
    out_ref[0, piece : piece + rows] = k_ref[...]
    out_ref[0, piece + rows :] = v_ref[...]


def pack_heads(queries, self_keys, self_values, devices):
    rows, features = queries.shape
    repeats = devices // (features // HEAD)
    piece = rows // repeats
    whole = pl.BlockSpec((rows, HEAD), lambda d: (0, d // repeats))
    return pl.pallas_call(
        pack_heads_kernel,
        grid=(devices,),
        out_shape=jax.ShapeDtypeStruct((devices, piece + 2 * rows, HEAD), BF16),
        in_specs=[
            pl.BlockSpec((piece, HEAD), lambda d: (d % repeats, d // repeats)),
            whole,
            whole,
        ],
        out_specs=pl.BlockSpec((1, piece + 2 * rows, HEAD), lambda d: (d, 0, 0)),
    )(queries, self_keys, self_values)


def attend_kernel(rows, rep_ref, data_ref, out_ref):
    source = pl.program_id(0)
    piece = out_ref.shape[1]
    query = data_ref[source, :piece]

    def scores_of(j):
        keys = data_ref[j, piece : piece + rows]
        return lax.dot_general(
            query, keys, (((1,), (1,)), ((), ())), preferred_element_type=F32
        ) * (SCALE * LOG2E)

    def mix(j, weights):
        return jnp.dot(
            weights.astype(BF16), data_ref[j, piece + rows :], preferred_element_type=F32
        )

    first = rep_ref[0] * piece
    row_ids = first + lax.broadcasted_iota(jnp.int32, (piece, rows), 0)
    col_ids = lax.broadcasted_iota(jnp.int32, (piece, rows), 1)
    scores = jnp.where(row_ids >= col_ids, scores_of(source), NEG_FILL)
    top = jnp.max(scores, axis=1, keepdims=True)
    weights = jnp.exp2(scores - top)
    total = jnp.sum(weights, axis=1, keepdims=True)
    acc = mix(source, weights)

    def body(j, state):
        top, total, acc = state
        scores = scores_of(j)
        newest = jnp.maximum(top, jnp.max(scores, axis=1, keepdims=True))
        weights = jnp.exp2(scores - newest)
        factor = jnp.exp2(top - newest)
        total = total * factor + jnp.sum(weights, axis=1, keepdims=True)
        return newest, total, acc * factor + mix(j, weights)

    top, total, acc = lax.fori_loop(0, source, body, (top, total, acc))
    out_ref[0] = (acc / total).astype(BF16)


def attend(data, rows):
    devices, height, _ = data.shape
    piece = height - 2 * rows
    heads = devices * piece // rows
    rep = (lax.axis_index("seq") % (rows // piece)).astype(jnp.int32).reshape(1)
    del heads
    return pl.pallas_call(
        functools.partial(attend_kernel, rows),
        grid_spec=pltpu.PrefetchScalarGridSpec(
            num_scalar_prefetch=1,
            grid=(devices,),
            in_specs=[pl.BlockSpec((devices, height, HEAD), lambda s, r: (0, 0, 0))],
            out_specs=pl.BlockSpec((1, piece, HEAD), lambda s, r: (s, 0, 0)),
        ),
        out_shape=jax.ShapeDtypeStruct((devices, piece, HEAD), BF16),
        compiler_params=pltpu.CompilerParams(vmem_limit_bytes=48 * 2**20),
    )(rep, data)


def ask_kernel(capacity, idx_ref, slot_ref, *refs):
    out_ref = refs[-1]
    dest = pl.program_id(0)
    lanes = lax.broadcasted_iota(jnp.int32, (INFO, out_ref.shape[2]), 1)
    info = jnp.zeros(lanes.shape, jnp.int32)
    for item in range(capacity):
        out_ref[0, item * SPAN : (item + 1) * SPAN] = refs[item][...]
        info = jnp.where(lanes == item, slot_ref[dest * capacity + item], info)
    out_ref[0, capacity * SPAN :] = info.astype(F32).astype(BF16)


def ask(cross_query, indices, slots, devices, capacity):
    features = cross_query.shape[1]
    height = capacity * SPAN + INFO
    return pl.pallas_call(
        functools.partial(ask_kernel, capacity),
        grid_spec=pltpu.PrefetchScalarGridSpec(
            num_scalar_prefetch=2,
            grid=(devices,),
            in_specs=[
                pl.BlockSpec(
                    (SPAN, features), lambda d, i, s, item=item: (i[d * capacity + item], 0)
                )
                for item in range(capacity)
            ],
            out_specs=pl.BlockSpec((1, height, features), lambda d, i, s: (d, 0, 0)),
        ),
        out_shape=jax.ShapeDtypeStruct((devices, height, features), BF16),
    )(indices, slots, *([cross_query] * capacity))


def answer_kernel(capacity, want_ref, asked_ref, *refs):
    out_ref = refs[-1]
    features = out_ref.shape[2]
    heads = features // HEAD
    lanes = lax.broadcasted_iota(jnp.int32, (SPAN, HEAD), 1)
    logs = []
    for item in range(capacity):
        keys_ref, values_ref = refs[item], refs[capacity + item]
        rows = slice(item * SPAN, (item + 1) * SPAN)
        info = jnp.zeros((SPAN, HEAD), F32)
        for head in range(heads):
            cols = slice(head * HEAD, (head + 1) * HEAD)
            scores = (
                lax.dot_general(
                    asked_ref[0, rows, cols],
                    keys_ref[0, :, cols],
                    (((1,), (1,)), ((), ())),
                    preferred_element_type=F32,
                )
                * SCALE
            )
            top = jnp.max(scores, axis=1, keepdims=True)
            weights = jnp.exp(scores - top)
            mass = jnp.sum(weights, axis=1, keepdims=True)
            blended = jnp.dot(
                weights.astype(BF16), values_ref[0, :, cols], preferred_element_type=F32
            )
            out_ref[0, rows, cols] = (blended / mass).astype(BF16)
            log_mass = top + jnp.log(mass)
            coarse = log_mass.astype(BF16).astype(F32)
            info = jnp.where(lanes == head, coarse, info)
            info = jnp.where(lanes == heads + head, log_mass - coarse, info)
        logs.append(info)
    turned = jnp.transpose(jnp.concatenate(logs, axis=0))
    out_ref[0, capacity * SPAN :] = jnp.zeros((INFO, features), BF16)
    out_ref[0, capacity * SPAN :, : capacity * SPAN] = turned[:INFO].astype(BF16)


def answer(asked, wanted, memory_keys, memory_values, capacity):
    devices, height, features = asked.shape
    length = memory_keys.shape[1]
    tiles = [
        pl.BlockSpec(
            (1, length, features), lambda s, w, item=item: (w[s * capacity + item], 0, 0)
        )
        for item in range(capacity)
    ]
    block = pl.BlockSpec((1, height, features), lambda s, w: (s, 0, 0))
    return pl.pallas_call(
        functools.partial(answer_kernel, capacity),
        grid_spec=pltpu.PrefetchScalarGridSpec(
            num_scalar_prefetch=1,
            grid=(devices,),
            in_specs=[block] + tiles + tiles,
            out_specs=block,
        ),
        out_shape=jax.ShapeDtypeStruct((devices, height, features), BF16),
    )(wanted, asked, *([memory_keys] * capacity), *([memory_values] * capacity))


def combine_kernel(picks, capacity, owner_ref, rank_ref, *refs):
    out_ref = refs[-1]
    span = pl.program_id(0)
    features = out_ref.shape[1]
    heads = features // HEAD
    starts, logs = [], []
    for n in range(picks):
        rank = rank_ref[span * picks + n]
        starts.append(pl.multiple_of(rank * SPAN, SPAN))
        info = refs[n][0, capacity * SPAN :, : capacity * SPAN].astype(F32)
        turned = jnp.transpose(info)
        chosen = turned[:SPAN]
        for item in range(1, capacity):
            chosen = jnp.where(rank == item, turned[item * SPAN : (item + 1) * SPAN], chosen)
        logs.append(chosen)
    for head in range(heads):
        cols = slice(head * HEAD, (head + 1) * HEAD)
        masses = [c[:, head : head + 1] + c[:, heads + head : heads + head + 1] for c in logs]
        best = functools.reduce(jnp.maximum, masses)
        shares = [jnp.exp(m - best) for m in masses]
        whole = sum(shares)
        mixed = sum(
            share * refs[n][0, pl.ds(starts[n], SPAN), cols].astype(F32)
            for n, share in enumerate(shares)
        )
        out_ref[:, cols] = (mixed / whole).astype(BF16)


def combine(answers, owners, ranks, span_count, picks, capacity):
    devices, height, features = answers.shape
    return pl.pallas_call(
        functools.partial(combine_kernel, picks, capacity),
        grid_spec=pltpu.PrefetchScalarGridSpec(
            num_scalar_prefetch=2,
            grid=(span_count,),
            in_specs=[
                pl.BlockSpec(
                    (1, height, features), lambda c, o, r, n=n: (o[c * picks + n], 0, 0)
                )
                for n in range(picks)
            ],
            out_specs=pl.BlockSpec((SPAN, features), lambda c, o, r: (c, 0)),
        ),
        out_shape=jax.ShapeDtypeStruct((span_count * SPAN, features), BF16),
    )(owners, ranks, *([answers] * picks))


def exchange(value):
    return lax.all_to_all(value, "seq", split_axis=0, concat_axis=0, tiled=True)


def reduce_scatter(partial_value):
    groups = lax.axis_size("mp")
    own = lax.axis_index("mp")
    rows, width = partial_value.shape
    share = width // groups
    blocks = partial_value.reshape(rows, groups // 2, 2, share)
    core = own % 2
    kept = lax.dynamic_index_in_dim(blocks, core, 2, keepdims=False)
    given = lax.dynamic_index_in_dim(blocks, 1 - core, 2, keepdims=False).astype(BF16)
    got = lax.ppermute(given, "mp", [(i, i ^ 1) for i in range(groups)])
    kept = kept + got.astype(F32)
    mine = lax.dynamic_index_in_dim(kept, own // 2, 1, keepdims=False)
    for step in range(1, groups // 2):
        other = lax.dynamic_index_in_dim(kept, (own // 2) ^ step, 1, keepdims=False)
        came = lax.ppermute(
            other.astype(BF16), "mp", [(i, i ^ (2 * step)) for i in range(groups)]
        )
        mine = mine + came.astype(F32)
    return mine.astype(BF16)


def per_device(
    queries,
    self_keys,
    self_values,
    cross_query,
    memory_keys,
    memory_values,
    neighbour_owner,
    neighbour_slot,
    out_weight,
    cross_weight,
):
    devices = lax.axis_size("seq")
    rows, features = queries.shape
    heads = features // HEAD
    span_count, picks = neighbour_owner.shape
    requests = span_count * picks
    capacity = max(2, (requests + devices - 1) // devices)

    owners = neighbour_owner.reshape(requests)
    slots = neighbour_slot.reshape(requests)
    order = jnp.arange(requests, dtype=jnp.int32)
    ranks = jnp.sum(
        ((owners[:, None] == owners[None, :]) & (order[None, :] < order[:, None])).astype(
            jnp.int32
        ),
        axis=1,
    )
    target = owners * capacity + ranks
    hits = target[None, :] == jnp.arange(devices * capacity, dtype=jnp.int32)[:, None]
    indices = jnp.sum(jnp.where(hits, order[None, :] // picks, 0), axis=1)
    sent_slots = jnp.sum(jnp.where(hits, slots[None, :], 0), axis=1)

    asked = exchange(ask(cross_query, indices, sent_slots, devices, capacity))
    data = exchange(pack_heads(queries, self_keys, self_values, devices))
    wanted = asked[:, capacity * SPAN, :capacity].astype(jnp.int32).reshape(devices * capacity)
    answers = exchange(answer(asked, wanted, memory_keys, memory_values, capacity))
    attended = exchange(attend(data, rows))
    retrieved = combine(answers, owners, ranks, span_count, picks, capacity)
    piece = attended.shape[1]
    attended = jnp.transpose(
        attended.reshape(heads, rows // piece, piece, HEAD), (1, 2, 0, 3)
    ).reshape(rows, features)

    partial_value = jnp.dot(attended, out_weight, preferred_element_type=F32)
    partial_value = partial_value + jnp.dot(
        retrieved, cross_weight, preferred_element_type=F32
    )
    return reduce_scatter(partial_value)


def solution(mesh):
    placed = (
        P("seq", "mp"),
        P("seq", "mp"),
        P("seq", "mp"),
        P("seq", "mp"),
        P("seq", None, "mp"),
        P("seq", None, "mp"),
        P("seq", None),
        P("seq", None),
        P("mp", None),
        P("mp", None),
    )
    return jax.shard_map(
        per_device, mesh=mesh, in_specs=placed, out_specs=P("seq", "mp"), check_vma=False
    )
```

```python
import functools
import math

import jax
import jax.numpy as jnp
from jax import lax
from jax.experimental import pallas as pl
from jax.experimental.pallas import tpu as pltpu
from jax.sharding import PartitionSpec as P

HEAD = 128
SPAN = 64
NEG_FILL = -1e30
SCALE = HEAD ** (-0.5)
LOG2E = math.log2(math.e)
INFO = 16
F32 = jnp.float32
BF16 = jnp.bfloat16


def pack_heads_kernel(q_ref, k_ref, v_ref, out_ref):
    piece = q_ref.shape[0]
    rows = k_ref.shape[0]
    out_ref[0, :piece] = q_ref[...]
    out_ref[0, piece : piece + rows] = k_ref[...]
    out_ref[0, piece + rows :] = v_ref[...]


def pack_heads(queries, self_keys, self_values, devices):
    rows, features = queries.shape
    repeats = devices // (features // HEAD)
    piece = rows // repeats
    whole = pl.BlockSpec((rows, HEAD), lambda d: (0, d // repeats))
    return pl.pallas_call(
        pack_heads_kernel,
        grid=(devices,),
        out_shape=jax.ShapeDtypeStruct((devices, piece + 2 * rows, HEAD), BF16),
        in_specs=[
            pl.BlockSpec((piece, HEAD), lambda d: (d % repeats, d // repeats)),
            whole,
            whole,
        ],
        out_specs=pl.BlockSpec((1, piece + 2 * rows, HEAD), lambda d: (d, 0, 0)),
    )(queries, self_keys, self_values)


def attend_kernel(rows, rep_ref, data_ref, out_ref):
    source = pl.program_id(0)
    piece = out_ref.shape[1]
    query = data_ref[source, :piece]

    def scores_of(j):
        keys = data_ref[j, piece : piece + rows]
        return lax.dot_general(
            query, keys, (((1,), (1,)), ((), ())), preferred_element_type=F32
        ) * (SCALE * LOG2E)

    def mix(j, weights):
        return jnp.dot(
            weights.astype(BF16), data_ref[j, piece + rows :], preferred_element_type=F32
        )

    first = rep_ref[0] * piece
    row_ids = first + lax.broadcasted_iota(jnp.int32, (piece, rows), 0)
    col_ids = lax.broadcasted_iota(jnp.int32, (piece, rows), 1)
    scores = jnp.where(row_ids >= col_ids, scores_of(source), NEG_FILL)
    top = jnp.max(scores, axis=1, keepdims=True)
    weights = jnp.exp2(scores - top)
    total = jnp.sum(weights, axis=1, keepdims=True)
    acc = mix(source, weights)

    def body(j, state):
        top, total, acc = state
        scores = scores_of(j)
        newest = jnp.maximum(top, jnp.max(scores, axis=1, keepdims=True))
        weights = jnp.exp2(scores - newest)
        factor = jnp.exp2(top - newest)
        total = total * factor + jnp.sum(weights, axis=1, keepdims=True)
        return newest, total, acc * factor + mix(j, weights)

    top, total, acc = lax.fori_loop(0, source, body, (top, total, acc))
    out_ref[0] = (acc / total).astype(BF16)


def attend(data, rows):
    devices, height, _ = data.shape
    piece = height - 2 * rows
    heads = devices * piece // rows
    rep = (lax.axis_index("seq") % (rows // piece)).astype(jnp.int32).reshape(1)
    del heads
    return pl.pallas_call(
        functools.partial(attend_kernel, rows),
        grid_spec=pltpu.PrefetchScalarGridSpec(
            num_scalar_prefetch=1,
            grid=(devices,),
            in_specs=[pl.BlockSpec((devices, height, HEAD), lambda s, r: (0, 0, 0))],
            out_specs=pl.BlockSpec((1, piece, HEAD), lambda s, r: (s, 0, 0)),
        ),
        out_shape=jax.ShapeDtypeStruct((devices, piece, HEAD), BF16),
        compiler_params=pltpu.CompilerParams(vmem_limit_bytes=48 * 2**20),
    )(rep, data)


def ask_kernel(capacity, idx_ref, slot_ref, *refs):
    out_ref = refs[-1]
    dest = pl.program_id(0)
    lanes = lax.broadcasted_iota(jnp.int32, (INFO, out_ref.shape[2]), 1)
    info = jnp.zeros(lanes.shape, jnp.int32)
    for item in range(capacity):
        out_ref[0, item * SPAN : (item + 1) * SPAN] = refs[item][...]
        info = jnp.where(lanes == item, slot_ref[dest * capacity + item], info)
    out_ref[0, capacity * SPAN :] = info.astype(F32).astype(BF16)


def ask(cross_query, indices, slots, devices, capacity):
    features = cross_query.shape[1]
    height = capacity * SPAN + INFO
    return pl.pallas_call(
        functools.partial(ask_kernel, capacity),
        grid_spec=pltpu.PrefetchScalarGridSpec(
            num_scalar_prefetch=2,
            grid=(devices,),
            in_specs=[
                pl.BlockSpec(
                    (SPAN, features), lambda d, i, s, item=item: (i[d * capacity + item], 0)
                )
                for item in range(capacity)
            ],
            out_specs=pl.BlockSpec((1, height, features), lambda d, i, s: (d, 0, 0)),
        ),
        out_shape=jax.ShapeDtypeStruct((devices, height, features), BF16),
    )(indices, slots, *([cross_query] * capacity))


def answer_kernel(capacity, want_ref, asked_ref, *refs):
    out_ref = refs[-1]
    features = out_ref.shape[2]
    heads = features // HEAD
    lanes = lax.broadcasted_iota(jnp.int32, (SPAN, HEAD), 1)
    logs = []
    for item in range(capacity):
        keys_ref, values_ref = refs[item], refs[capacity + item]
        rows = slice(item * SPAN, (item + 1) * SPAN)
        info = jnp.zeros((SPAN, HEAD), F32)
        for head in range(heads):
            cols = slice(head * HEAD, (head + 1) * HEAD)
            scores = (
                lax.dot_general(
                    asked_ref[0, rows, cols],
                    keys_ref[0, :, cols],
                    (((1,), (1,)), ((), ())),
                    preferred_element_type=F32,
                )
                * SCALE
            )
            top = jnp.max(scores, axis=1, keepdims=True)
            weights = jnp.exp(scores - top)
            mass = jnp.sum(weights, axis=1, keepdims=True)
            blended = jnp.dot(
                weights.astype(BF16), values_ref[0, :, cols], preferred_element_type=F32
            )
            out_ref[0, rows, cols] = (blended / mass).astype(BF16)
            log_mass = top + jnp.log(mass)
            coarse = log_mass.astype(BF16).astype(F32)
            info = jnp.where(lanes == head, coarse, info)
            info = jnp.where(lanes == heads + head, log_mass - coarse, info)
        logs.append(info)
    turned = jnp.transpose(jnp.concatenate(logs, axis=0))
    out_ref[0, capacity * SPAN :] = jnp.zeros((INFO, features), BF16)
    out_ref[0, capacity * SPAN :, : capacity * SPAN] = turned[:INFO].astype(BF16)


def answer(asked, wanted, memory_keys, memory_values, capacity):
    devices, height, features = asked.shape
    length = memory_keys.shape[1]
    tiles = [
        pl.BlockSpec(
            (1, length, features), lambda s, w, item=item: (w[s * capacity + item], 0, 0)
        )
        for item in range(capacity)
    ]
    block = pl.BlockSpec((1, height, features), lambda s, w: (s, 0, 0))
    return pl.pallas_call(
        functools.partial(answer_kernel, capacity),
        grid_spec=pltpu.PrefetchScalarGridSpec(
            num_scalar_prefetch=1,
            grid=(devices,),
            in_specs=[block] + tiles + tiles,
            out_specs=block,
        ),
        out_shape=jax.ShapeDtypeStruct((devices, height, features), BF16),
    )(wanted, asked, *([memory_keys] * capacity), *([memory_values] * capacity))


def combine_kernel(picks, capacity, owner_ref, rank_ref, *refs):
    out_ref = refs[-1]
    span = pl.program_id(0)
    features = out_ref.shape[1]
    heads = features // HEAD
    starts, logs = [], []
    for n in range(picks):
        rank = rank_ref[span * picks + n]
        starts.append(pl.multiple_of(rank * SPAN, SPAN))
        info = refs[n][0, capacity * SPAN :, : capacity * SPAN].astype(F32)
        turned = jnp.transpose(info)
        chosen = turned[:SPAN]
        for item in range(1, capacity):
            chosen = jnp.where(rank == item, turned[item * SPAN : (item + 1) * SPAN], chosen)
        logs.append(chosen)
    for head in range(heads):
        cols = slice(head * HEAD, (head + 1) * HEAD)
        masses = [c[:, head : head + 1] + c[:, heads + head : heads + head + 1] for c in logs]
        best = functools.reduce(jnp.maximum, masses)
        shares = [jnp.exp(m - best) for m in masses]
        whole = sum(shares)
        mixed = sum(
            share * refs[n][0, pl.ds(starts[n], SPAN), cols].astype(F32)
            for n, share in enumerate(shares)
        )
        out_ref[:, cols] = (mixed / whole).astype(BF16)


def combine(answers, owners, ranks, span_count, picks, capacity):
    devices, height, features = answers.shape
    return pl.pallas_call(
        functools.partial(combine_kernel, picks, capacity),
        grid_spec=pltpu.PrefetchScalarGridSpec(
            num_scalar_prefetch=2,
            grid=(span_count,),
            in_specs=[
                pl.BlockSpec(
                    (1, height, features), lambda c, o, r, n=n: (o[c * picks + n], 0, 0)
                )
                for n in range(picks)
            ],
            out_specs=pl.BlockSpec((SPAN, features), lambda c, o, r: (c, 0)),
        ),
        out_shape=jax.ShapeDtypeStruct((span_count * SPAN, features), BF16),
    )(owners, ranks, *([answers] * picks))


def exchange(value):
    return lax.all_to_all(value, "seq", split_axis=0, concat_axis=0, tiled=True)


def project_kernel(block_ref, att_ref, ret_ref, out_weight_ref, cross_weight_ref, out_ref):
    total = jnp.dot(att_ref[...], out_weight_ref[...], preferred_element_type=F32)
    total += jnp.dot(ret_ref[...], cross_weight_ref[...], preferred_element_type=F32)
    out_ref[...] = total.astype(BF16)


def project(attended, retrieved, out_weight, cross_weight, block, width):
    rows, features = attended.shape
    tiles = 2
    tile = width // tiles
    left = pl.BlockSpec((rows, features), lambda t, b: (0, 0))
    right = pl.BlockSpec((features, tile), lambda t, b: (0, b[0] * tiles + t))
    return pl.pallas_call(
        project_kernel,
        grid_spec=pltpu.PrefetchScalarGridSpec(
            num_scalar_prefetch=1,
            grid=(tiles,),
            in_specs=[left, left, right, right],
            out_specs=pl.BlockSpec((rows, tile), lambda t, b: (0, t)),
        ),
        out_shape=jax.ShapeDtypeStruct((rows, width), BF16),
        cost_estimate=pl.CostEstimate(
            flops=4 * rows * features * width,
            bytes_accessed=2 * (2 * features * width + rows * (2 * features + width)),
            transcendentals=0,
        ),
    )(block.astype(jnp.int32).reshape(1), attended, retrieved, out_weight, cross_weight)


def project_and_sum(attended, retrieved, out_weight, cross_weight):
    groups = lax.axis_size("mp")
    own = lax.axis_index("mp")
    share = out_weight.shape[1] // groups
    core, chip = own % 2, own // 2
    came = []
    for step in range(groups // 2 - 1, -1, -1):
        pair = 2 * (chip ^ step)
        given = project(attended, retrieved, out_weight, cross_weight, pair + 1 - core, share)
        got = lax.ppermute(given, "mp", [(i, i ^ 1) for i in range(groups)])
        kept = project(attended, retrieved, out_weight, cross_weight, pair + core, share)
        total = kept.astype(F32) + got.astype(F32)
        if step:
            total, attended = lax.optimization_barrier((total.astype(BF16), attended))
            came.append(
                lax.ppermute(total, "mp", [(i, i ^ (2 * step)) for i in range(groups)])
            )
    for other in came:
        total = total + other.astype(F32)
    return total.astype(BF16)


def per_device(
    queries,
    self_keys,
    self_values,
    cross_query,
    memory_keys,
    memory_values,
    neighbour_owner,
    neighbour_slot,
    out_weight,
    cross_weight,
):
    devices = lax.axis_size("seq")
    rows, features = queries.shape
    heads = features // HEAD
    span_count, picks = neighbour_owner.shape
    requests = span_count * picks
    capacity = max(2, (requests + devices - 1) // devices)

    owners = neighbour_owner.reshape(requests)
    slots = neighbour_slot.reshape(requests)
    order = jnp.arange(requests, dtype=jnp.int32)
    ranks = jnp.sum(
        ((owners[:, None] == owners[None, :]) & (order[None, :] < order[:, None])).astype(
            jnp.int32
        ),
        axis=1,
    )
    target = owners * capacity + ranks
    hits = target[None, :] == jnp.arange(devices * capacity, dtype=jnp.int32)[:, None]
    indices = jnp.sum(jnp.where(hits, order[None, :] // picks, 0), axis=1)
    sent_slots = jnp.sum(jnp.where(hits, slots[None, :], 0), axis=1)

    asked = exchange(ask(cross_query, indices, sent_slots, devices, capacity))
    packed = pack_heads(queries, self_keys, self_values, devices)
    asked, packed = lax.optimization_barrier((asked, packed))
    data = exchange(packed)
    wanted = asked[:, capacity * SPAN, :capacity].astype(jnp.int32).reshape(devices * capacity)
    answered = answer(asked, wanted, memory_keys, memory_values, capacity)
    data, answered = lax.optimization_barrier((data, answered))
    answers = exchange(answered)
    attended = attend(data, rows)
    answers, attended = lax.optimization_barrier((answers, attended))
    attended = exchange(attended)
    retrieved = combine(answers, owners, ranks, span_count, picks, capacity)
    piece = attended.shape[1]
    attended = jnp.transpose(
        attended.reshape(heads, rows // piece, piece, HEAD), (1, 2, 0, 3)
    ).reshape(rows, features)
    return project_and_sum(attended, retrieved, out_weight, cross_weight)


def solution(mesh):
    placed = (
        P("seq", "mp"),
        P("seq", "mp"),
        P("seq", "mp"),
        P("seq", "mp"),
        P("seq", None, "mp"),
        P("seq", None, "mp"),
        P("seq", None),
        P("seq", None),
        P("mp", None),
        P("mp", None),
    )
    return jax.shard_map(
        per_device, mesh=mesh, in_specs=placed, out_specs=P("seq", "mp"), check_vma=False
    )
```

```python
import functools
import math

import jax
import jax.numpy as jnp
from jax import lax
from jax.experimental import pallas as pl
from jax.experimental.pallas import tpu as pltpu
from jax.sharding import PartitionSpec as P

HEAD = 128
SPAN = 64
NEG_FILL = -1e30
SCALE = HEAD ** (-0.5)
LOG2E = math.log2(math.e)
INFO = 16
F32 = jnp.float32
BF16 = jnp.bfloat16


def pack_heads_kernel(q_ref, k_ref, v_ref, out_ref):
    out_ref[0, 0] = q_ref[...]
    out_ref[0, 1] = k_ref[...]
    out_ref[0, 2] = v_ref[...]


def pack_heads(queries, self_keys, self_values, devices):
    rows, features = queries.shape
    repeats = devices // (features // HEAD)
    piece = rows // repeats
    part = pl.BlockSpec((piece, HEAD), lambda d: (d % repeats, d // repeats))
    return pl.pallas_call(
        pack_heads_kernel,
        grid=(devices,),
        out_shape=jax.ShapeDtypeStruct((devices, 3, piece, HEAD), BF16),
        in_specs=[part] * 3,
        out_specs=pl.BlockSpec((1, 3, piece, HEAD), lambda d: (d, 0, 0, 0)),
    )(queries, self_keys, self_values)


def attend_kernel(repeats, rep_ref, *refs):
    out_ref = refs[-1]
    source = pl.program_id(0)
    piece = out_ref.shape[1]
    query = refs[0][source, 0]

    def scores_of(turn, j):
        return lax.dot_general(
            query, refs[turn][j, -2 % refs[turn].shape[1]], (((1,), (1,)), ((), ())), preferred_element_type=F32
        ) * (SCALE * LOG2E)

    def mix(turn, j, weights):
        return jnp.dot(weights.astype(BF16), refs[turn][j, -1 % refs[turn].shape[1]], preferred_element_type=F32)

    def fold(j, all_scores, state):
        tops = [jnp.max(scores, axis=1, keepdims=True) for scores in all_scores]
        newest = functools.reduce(jnp.maximum, tops)
        if state is not None:
            newest = jnp.maximum(newest, state[0])
        weights = [jnp.exp2(scores - newest) for scores in all_scores]
        total = sum(jnp.sum(part, axis=1, keepdims=True) for part in weights)
        acc = sum(mix(turn, j, part) for turn, part in enumerate(weights))
        if state is not None:
            factor = jnp.exp2(state[0] - newest)
            total += state[1] * factor
            acc += state[2] * factor
        return newest, total, acc

    rep = rep_ref[0]
    row_ids = lax.broadcasted_iota(jnp.int32, (piece, piece), 0)
    col_ids = lax.broadcasted_iota(jnp.int32, (piece, piece), 1)
    diagonal = []
    for turn in range(repeats):
        ahead = (rep - lax.rem(rep + repeats - turn, repeats)) * piece
        diagonal.append(
            jnp.where(row_ids + ahead >= col_ids, scores_of(turn, source), NEG_FILL)
        )
    state = fold(source, diagonal, None)

    def body(j, state):
        return fold(j, [scores_of(turn, j) for turn in range(repeats)], state)

    _, total, acc = lax.fori_loop(0, source, body, state)
    out_ref[0] = (acc / total).astype(BF16)


def attend(data, repeats):
    devices, _, piece, _ = data.shape
    rep = (lax.axis_index("seq") % repeats).astype(jnp.int32).reshape(1)
    held = [data]
    for turn in range(1, repeats):
        pairs = [
            (i, i // repeats * repeats + (i + turn) % repeats) for i in range(devices)
        ]
        held.append(lax.ppermute(data[:, 1:], "seq", pairs))
    return pl.pallas_call(
        functools.partial(attend_kernel, repeats),
        grid_spec=pltpu.PrefetchScalarGridSpec(
            num_scalar_prefetch=1,
            grid=(devices,),
            in_specs=[pl.BlockSpec(part.shape, lambda s, r: (0, 0, 0, 0)) for part in held],
            out_specs=pl.BlockSpec((1, piece, HEAD), lambda s, r: (s, 0, 0)),
        ),
        out_shape=jax.ShapeDtypeStruct((devices, piece, HEAD), BF16),
        compiler_params=pltpu.CompilerParams(vmem_limit_bytes=48 * 2**20),
    )(rep, *held)


def ask_kernel(capacity, idx_ref, slot_ref, *refs):
    out_ref = refs[-1]
    dest = pl.program_id(0)
    lanes = lax.broadcasted_iota(jnp.int32, (INFO, out_ref.shape[2]), 1)
    info = jnp.zeros(lanes.shape, jnp.int32)
    for item in range(capacity):
        out_ref[0, item * SPAN : (item + 1) * SPAN] = refs[item][...]
        info = jnp.where(lanes == item, slot_ref[dest * capacity + item], info)
    out_ref[0, capacity * SPAN :] = info.astype(F32).astype(BF16)


def ask(cross_query, indices, slots, devices, capacity):
    features = cross_query.shape[1]
    height = capacity * SPAN + INFO
    return pl.pallas_call(
        functools.partial(ask_kernel, capacity),
        grid_spec=pltpu.PrefetchScalarGridSpec(
            num_scalar_prefetch=2,
            grid=(devices,),
            in_specs=[
                pl.BlockSpec(
                    (SPAN, features), lambda d, i, s, item=item: (i[d * capacity + item], 0)
                )
                for item in range(capacity)
            ],
            out_specs=pl.BlockSpec((1, height, features), lambda d, i, s: (d, 0, 0)),
        ),
        out_shape=jax.ShapeDtypeStruct((devices, height, features), BF16),
    )(indices, slots, *([cross_query] * capacity))


def answer_kernel(capacity, want_ref, asked_ref, *refs):
    out_ref = refs[-1]
    features = out_ref.shape[2]
    heads = features // HEAD
    lanes = lax.broadcasted_iota(jnp.int32, (SPAN, HEAD), 1)
    logs = []
    for item in range(capacity):
        keys_ref, values_ref = refs[item], refs[capacity + item]
        rows = slice(item * SPAN, (item + 1) * SPAN)
        info = jnp.zeros((SPAN, HEAD), F32)
        for head in range(heads):
            cols = slice(head * HEAD, (head + 1) * HEAD)
            scores = (
                lax.dot_general(
                    asked_ref[0, rows, cols],
                    keys_ref[0, :, cols],
                    (((1,), (1,)), ((), ())),
                    preferred_element_type=F32,
                )
                * SCALE
            )
            top = jnp.max(scores, axis=1, keepdims=True)
            weights = jnp.exp(scores - top)
            mass = jnp.sum(weights, axis=1, keepdims=True)
            blended = jnp.dot(
                weights.astype(BF16), values_ref[0, :, cols], preferred_element_type=F32
            )
            out_ref[0, rows, cols] = (blended / mass).astype(BF16)
            log_mass = top + jnp.log(mass)
            coarse = log_mass.astype(BF16).astype(F32)
            info = jnp.where(lanes == head, coarse, info)
            info = jnp.where(lanes == heads + head, log_mass - coarse, info)
        logs.append(info)
    turned = jnp.transpose(jnp.concatenate(logs, axis=0))
    out_ref[0, capacity * SPAN :] = jnp.zeros((INFO, features), BF16)
    out_ref[0, capacity * SPAN :, : capacity * SPAN] = turned[:INFO].astype(BF16)


def answer(asked, wanted, memory_keys, memory_values, capacity):
    devices, height, features = asked.shape
    length = memory_keys.shape[1]
    tiles = [
        pl.BlockSpec(
            (1, length, features), lambda s, w, item=item: (w[s * capacity + item], 0, 0)
        )
        for item in range(capacity)
    ]
    block = pl.BlockSpec((1, height, features), lambda s, w: (s, 0, 0))
    return pl.pallas_call(
        functools.partial(answer_kernel, capacity),
        grid_spec=pltpu.PrefetchScalarGridSpec(
            num_scalar_prefetch=1,
            grid=(devices,),
            in_specs=[block] + tiles + tiles,
            out_specs=block,
        ),
        out_shape=jax.ShapeDtypeStruct((devices, height, features), BF16),
    )(wanted, asked, *([memory_keys] * capacity), *([memory_values] * capacity))


def combine_kernel(picks, capacity, owner_ref, rank_ref, *refs):
    out_ref = refs[-1]
    span = pl.program_id(0)
    features = out_ref.shape[1]
    heads = features // HEAD
    starts, logs = [], []
    for n in range(picks):
        rank = rank_ref[span * picks + n]
        starts.append(pl.multiple_of(rank * SPAN, SPAN))
        info = refs[n][0, capacity * SPAN :, : capacity * SPAN].astype(F32)
        turned = jnp.transpose(info)
        chosen = turned[:SPAN]
        for item in range(1, capacity):
            chosen = jnp.where(rank == item, turned[item * SPAN : (item + 1) * SPAN], chosen)
        logs.append(chosen)
    for head in range(heads):
        cols = slice(head * HEAD, (head + 1) * HEAD)
        masses = [c[:, head : head + 1] + c[:, heads + head : heads + head + 1] for c in logs]
        best = functools.reduce(jnp.maximum, masses)
        shares = [jnp.exp(m - best) for m in masses]
        whole = sum(shares)
        mixed = sum(
            share * refs[n][0, pl.ds(starts[n], SPAN), cols].astype(F32)
            for n, share in enumerate(shares)
        )
        out_ref[:, cols] = (mixed / whole).astype(BF16)


def combine(answers, owners, ranks, span_count, picks, capacity):
    devices, height, features = answers.shape
    return pl.pallas_call(
        functools.partial(combine_kernel, picks, capacity),
        grid_spec=pltpu.PrefetchScalarGridSpec(
            num_scalar_prefetch=2,
            grid=(span_count,),
            in_specs=[
                pl.BlockSpec(
                    (1, height, features), lambda c, o, r, n=n: (o[c * picks + n], 0, 0)
                )
                for n in range(picks)
            ],
            out_specs=pl.BlockSpec((SPAN, features), lambda c, o, r: (c, 0)),
        ),
        out_shape=jax.ShapeDtypeStruct((span_count * SPAN, features), BF16),
    )(owners, ranks, *([answers] * picks))


def exchange(value):
    return lax.all_to_all(value, "seq", split_axis=0, concat_axis=0, tiled=True)


def project_kernel(block_ref, att_ref, ret_ref, out_weight_ref, cross_weight_ref, out_ref):
    total = jnp.dot(att_ref[...], out_weight_ref[...], preferred_element_type=F32)
    total += jnp.dot(ret_ref[...], cross_weight_ref[...], preferred_element_type=F32)
    out_ref[...] = total.astype(BF16)


def project(attended, retrieved, out_weight, cross_weight, block, width):
    rows, features = attended.shape
    tiles = 2
    tile = width // tiles
    left = pl.BlockSpec((rows, features), lambda t, b: (0, 0))
    right = pl.BlockSpec((features, tile), lambda t, b: (0, b[0] * tiles + t))
    return pl.pallas_call(
        project_kernel,
        grid_spec=pltpu.PrefetchScalarGridSpec(
            num_scalar_prefetch=1,
            grid=(tiles,),
            in_specs=[left, left, right, right],
            out_specs=pl.BlockSpec((rows, tile), lambda t, b: (0, t)),
        ),
        out_shape=jax.ShapeDtypeStruct((rows, width), BF16),
        cost_estimate=pl.CostEstimate(
            flops=4 * rows * features * width,
            bytes_accessed=2 * (2 * features * width + rows * (2 * features + width)),
            transcendentals=0,
        ),
    )(block.astype(jnp.int32).reshape(1), attended, retrieved, out_weight, cross_weight)


def project_and_sum(attended, retrieved, out_weight, cross_weight):
    groups = lax.axis_size("mp")
    own = lax.axis_index("mp")
    share = out_weight.shape[1] // groups
    core, chip = own % 2, own // 2
    came = []
    for step in range(groups // 2 - 1, -1, -1):
        pair = 2 * (chip ^ step)
        given = project(attended, retrieved, out_weight, cross_weight, pair + 1 - core, share)
        got = lax.ppermute(given, "mp", [(i, i ^ 1) for i in range(groups)])
        kept = project(attended, retrieved, out_weight, cross_weight, pair + core, share)
        total = kept.astype(F32) + got.astype(F32)
        if step:
            total, attended = lax.optimization_barrier((total.astype(BF16), attended))
            came.append(
                lax.ppermute(total, "mp", [(i, i ^ (2 * step)) for i in range(groups)])
            )
    for other in came:
        total = total + other.astype(F32)
    return total.astype(BF16)


def per_device(
    queries,
    self_keys,
    self_values,
    cross_query,
    memory_keys,
    memory_values,
    neighbour_owner,
    neighbour_slot,
    out_weight,
    cross_weight,
):
    devices = lax.axis_size("seq")
    rows, features = queries.shape
    heads = features // HEAD
    span_count, picks = neighbour_owner.shape
    requests = span_count * picks
    capacity = max(2, (requests + devices - 1) // devices)

    owners = neighbour_owner.reshape(requests)
    slots = neighbour_slot.reshape(requests)
    order = jnp.arange(requests, dtype=jnp.int32)
    ranks = jnp.sum(
        ((owners[:, None] == owners[None, :]) & (order[None, :] < order[:, None])).astype(
            jnp.int32
        ),
        axis=1,
    )
    target = owners * capacity + ranks
    hits = target[None, :] == jnp.arange(devices * capacity, dtype=jnp.int32)[:, None]
    indices = jnp.sum(jnp.where(hits, order[None, :] // picks, 0), axis=1)
    sent_slots = jnp.sum(jnp.where(hits, slots[None, :], 0), axis=1)

    asked = exchange(ask(cross_query, indices, sent_slots, devices, capacity))
    packed = pack_heads(queries, self_keys, self_values, devices)
    asked, packed = lax.optimization_barrier((asked, packed))
    data = exchange(packed)
    wanted = asked[:, capacity * SPAN, :capacity].astype(jnp.int32).reshape(devices * capacity)
    answered = answer(asked, wanted, memory_keys, memory_values, capacity)
    data, answered = lax.optimization_barrier((data, answered))
    answers = exchange(answered)
    attended = attend(data, devices // heads)
    answers, attended = lax.optimization_barrier((answers, attended))
    attended = exchange(attended)
    retrieved = combine(answers, owners, ranks, span_count, picks, capacity)
    piece = attended.shape[1]
    attended = jnp.transpose(
        attended.reshape(heads, rows // piece, piece, HEAD), (1, 2, 0, 3)
    ).reshape(rows, features)
    return project_and_sum(attended, retrieved, out_weight, cross_weight)


def solution(mesh):
    placed = (
        P("seq", "mp"),
        P("seq", "mp"),
        P("seq", "mp"),
        P("seq", "mp"),
        P("seq", None, "mp"),
        P("seq", None, "mp"),
        P("seq", None),
        P("seq", None),
        P("mp", None),
        P("mp", None),
    )
    return jax.shard_map(
        per_device, mesh=mesh, in_specs=placed, out_specs=P("seq", "mp"), check_vma=False
    )
```

```python
import functools
import math

import jax
import jax.numpy as jnp
from jax import lax
from jax.experimental import pallas as pl
from jax.experimental.pallas import tpu as pltpu
from jax.sharding import PartitionSpec as P

HEAD = 128
SPAN = 64
NEG_FILL = -1e30
SCALE = HEAD ** (-0.5)
LOG2E = math.log2(math.e)
INFO = 16
F32 = jnp.float32
BF16 = jnp.bfloat16


def pack_heads_kernel(q_ref, k_ref, v_ref, out_ref):
    piece = q_ref.shape[0]
    rows = k_ref.shape[0]
    out_ref[0, :piece] = q_ref[...]
    out_ref[0, piece : piece + rows] = k_ref[...]
    out_ref[0, piece + rows :] = v_ref[...]


def pack_heads(queries, self_keys, self_values, devices):
    rows, features = queries.shape
    repeats = devices // (features // HEAD)
    piece = rows // repeats
    whole = pl.BlockSpec((rows, HEAD), lambda d: (0, d // repeats))
    return pl.pallas_call(
        pack_heads_kernel,
        grid=(devices,),
        out_shape=jax.ShapeDtypeStruct((devices, piece + 2 * rows, HEAD), BF16),
        in_specs=[
            pl.BlockSpec((piece, HEAD), lambda d: (d % repeats, d // repeats)),
            whole,
            whole,
        ],
        out_specs=pl.BlockSpec((1, piece + 2 * rows, HEAD), lambda d: (d, 0, 0)),
    )(queries, self_keys, self_values)


def attend_kernel(rows, rep_ref, data_ref, out_ref):
    source = pl.program_id(0)
    piece = out_ref.shape[1]
    query = data_ref[source, :piece]

    def scores_of(j):
        keys = data_ref[j, piece : piece + rows]
        return lax.dot_general(
            query, keys, (((1,), (1,)), ((), ())), preferred_element_type=F32
        ) * (SCALE * LOG2E)

    def mix(j, weights):
        return jnp.dot(
            weights.astype(BF16), data_ref[j, piece + rows :], preferred_element_type=F32
        )

    first = rep_ref[0] * piece
    row_ids = first + lax.broadcasted_iota(jnp.int32, (piece, rows), 0)
    col_ids = lax.broadcasted_iota(jnp.int32, (piece, rows), 1)
    scores = jnp.where(row_ids >= col_ids, scores_of(source), NEG_FILL)
    top = jnp.max(scores, axis=1, keepdims=True)
    weights = jnp.exp2(scores - top)
    total = jnp.sum(weights, axis=1, keepdims=True)
    acc = mix(source, weights)

    def body(j, state):
        top, total, acc = state
        scores = scores_of(j)
        newest = jnp.maximum(top, jnp.max(scores, axis=1, keepdims=True))
        weights = jnp.exp2(scores - newest)
        factor = jnp.exp2(top - newest)
        total = total * factor + jnp.sum(weights, axis=1, keepdims=True)
        return newest, total, acc * factor + mix(j, weights)

    top, total, acc = lax.fori_loop(0, source, body, (top, total, acc))
    out_ref[0] = (acc / total).astype(BF16)


def attend(data, rows):
    devices, height, _ = data.shape
    piece = height - 2 * rows
    heads = devices * piece // rows
    rep = (lax.axis_index("seq") % (rows // piece)).astype(jnp.int32).reshape(1)
    del heads
    return pl.pallas_call(
        functools.partial(attend_kernel, rows),
        grid_spec=pltpu.PrefetchScalarGridSpec(
            num_scalar_prefetch=1,
            grid=(devices,),
            in_specs=[pl.BlockSpec((devices, height, HEAD), lambda s, r: (0, 0, 0))],
            out_specs=pl.BlockSpec((1, piece, HEAD), lambda s, r: (s, 0, 0)),
        ),
        out_shape=jax.ShapeDtypeStruct((devices, piece, HEAD), BF16),
        compiler_params=pltpu.CompilerParams(vmem_limit_bytes=48 * 2**20),
    )(rep, data)


def ask_kernel(capacity, idx_ref, slot_ref, query_ref, out_ref):
    lanes = lax.broadcasted_iota(jnp.int32, (INFO, out_ref.shape[2]), 1)

    def body(dest, carry):
        info = jnp.zeros(lanes.shape, jnp.int32)
        for item in range(capacity):
            start = pl.multiple_of(idx_ref[dest * capacity + item] * SPAN, SPAN)
            out_ref[dest, item * SPAN : (item + 1) * SPAN] = query_ref[pl.ds(start, SPAN)]
            info = jnp.where(lanes == item, slot_ref[dest * capacity + item], info)
        out_ref[dest, capacity * SPAN :] = info.astype(F32).astype(BF16)
        return carry

    lax.fori_loop(0, out_ref.shape[0], body, 0)


def ask(cross_query, indices, slots, devices, capacity):
    features = cross_query.shape[1]
    height = capacity * SPAN + INFO
    return pl.pallas_call(
        functools.partial(ask_kernel, capacity),
        grid_spec=pltpu.PrefetchScalarGridSpec(
            num_scalar_prefetch=2,
            grid=(1,),
            in_specs=[pl.BlockSpec(cross_query.shape, lambda d, i, s: (0, 0))],
            out_specs=pl.BlockSpec((devices, height, features), lambda d, i, s: (0, 0, 0)),
        ),
        out_shape=jax.ShapeDtypeStruct((devices, height, features), BF16),
        compiler_params=pltpu.CompilerParams(vmem_limit_bytes=32 * 2**20),
    )(indices, slots, cross_query)


def answer_kernel(capacity, want_ref, asked_ref, *refs):
    out_ref = refs[-1]
    features = out_ref.shape[2]
    heads = features // HEAD
    lanes = lax.broadcasted_iota(jnp.int32, (SPAN, HEAD), 1)
    logs = []
    for item in range(capacity):
        keys_ref, values_ref = refs[item], refs[capacity + item]
        rows = slice(item * SPAN, (item + 1) * SPAN)
        info = jnp.zeros((SPAN, HEAD), F32)
        for head in range(heads):
            cols = slice(head * HEAD, (head + 1) * HEAD)
            scores = (
                lax.dot_general(
                    asked_ref[0, rows, cols],
                    keys_ref[0, :, cols],
                    (((1,), (1,)), ((), ())),
                    preferred_element_type=F32,
                )
                * SCALE
            )
            top = jnp.max(scores, axis=1, keepdims=True)
            weights = jnp.exp(scores - top)
            mass = jnp.sum(weights, axis=1, keepdims=True)
            blended = jnp.dot(
                weights.astype(BF16), values_ref[0, :, cols], preferred_element_type=F32
            )
            out_ref[0, rows, cols] = (blended / mass).astype(BF16)
            log_mass = top + jnp.log(mass)
            coarse = log_mass.astype(BF16).astype(F32)
            info = jnp.where(lanes == head, coarse, info)
            info = jnp.where(lanes == heads + head, log_mass - coarse, info)
        logs.append(info)
    turned = jnp.transpose(jnp.concatenate(logs, axis=0))
    out_ref[0, capacity * SPAN :] = jnp.zeros((INFO, features), BF16)
    out_ref[0, capacity * SPAN :, : capacity * SPAN] = turned[:INFO].astype(BF16)


def answer(asked, wanted, memory_keys, memory_values, capacity):
    devices, height, features = asked.shape
    length = memory_keys.shape[1]
    tiles = [
        pl.BlockSpec(
            (1, length, features), lambda s, w, item=item: (w[s * capacity + item], 0, 0)
        )
        for item in range(capacity)
    ]
    block = pl.BlockSpec((1, height, features), lambda s, w: (s, 0, 0))
    return pl.pallas_call(
        functools.partial(answer_kernel, capacity),
        grid_spec=pltpu.PrefetchScalarGridSpec(
            num_scalar_prefetch=1,
            grid=(devices,),
            in_specs=[block] + tiles + tiles,
            out_specs=block,
        ),
        out_shape=jax.ShapeDtypeStruct((devices, height, features), BF16),
    )(wanted, asked, *([memory_keys] * capacity), *([memory_values] * capacity))


def combine_kernel(picks, capacity, owner_ref, rank_ref, *refs):
    out_ref = refs[-1]
    span = pl.program_id(0)
    features = out_ref.shape[1]
    heads = features // HEAD
    starts, logs = [], []
    for n in range(picks):
        rank = rank_ref[span * picks + n]
        starts.append(pl.multiple_of(rank * SPAN, SPAN))
        info = refs[n][0, capacity * SPAN :, : capacity * SPAN].astype(F32)
        turned = jnp.transpose(info)
        chosen = turned[:SPAN]
        for item in range(1, capacity):
            chosen = jnp.where(rank == item, turned[item * SPAN : (item + 1) * SPAN], chosen)
        logs.append(chosen)
    for head in range(heads):
        cols = slice(head * HEAD, (head + 1) * HEAD)
        masses = [c[:, head : head + 1] + c[:, heads + head : heads + head + 1] for c in logs]
        best = functools.reduce(jnp.maximum, masses)
        shares = [jnp.exp(m - best) for m in masses]
        whole = sum(shares)
        mixed = sum(
            share * refs[n][0, pl.ds(starts[n], SPAN), cols].astype(F32)
            for n, share in enumerate(shares)
        )
        out_ref[:, cols] = (mixed / whole).astype(BF16)


def combine(answers, owners, ranks, span_count, picks, capacity):
    devices, height, features = answers.shape
    return pl.pallas_call(
        functools.partial(combine_kernel, picks, capacity),
        grid_spec=pltpu.PrefetchScalarGridSpec(
            num_scalar_prefetch=2,
            grid=(span_count,),
            in_specs=[
                pl.BlockSpec(
                    (1, height, features), lambda c, o, r, n=n: (o[c * picks + n], 0, 0)
                )
                for n in range(picks)
            ],
            out_specs=pl.BlockSpec((SPAN, features), lambda c, o, r: (c, 0)),
        ),
        out_shape=jax.ShapeDtypeStruct((span_count * SPAN, features), BF16),
    )(owners, ranks, *([answers] * picks))


def exchange(value):
    return lax.all_to_all(value, "seq", split_axis=0, concat_axis=0, tiled=True)


def project_kernel(block_ref, att_ref, ret_ref, out_weight_ref, cross_weight_ref, out_ref):
    total = jnp.dot(att_ref[...], out_weight_ref[...], preferred_element_type=F32)
    total += jnp.dot(ret_ref[...], cross_weight_ref[...], preferred_element_type=F32)
    out_ref[...] = total.astype(BF16)


def project(attended, retrieved, out_weight, cross_weight, block, width):
    rows, features = attended.shape
    tiles = 2
    tile = width // tiles
    left = pl.BlockSpec((rows, features), lambda t, b: (0, 0))
    right = pl.BlockSpec((features, tile), lambda t, b: (0, b[0] * tiles + t))
    return pl.pallas_call(
        project_kernel,
        grid_spec=pltpu.PrefetchScalarGridSpec(
            num_scalar_prefetch=1,
            grid=(tiles,),
            in_specs=[left, left, right, right],
            out_specs=pl.BlockSpec((rows, tile), lambda t, b: (0, t)),
        ),
        out_shape=jax.ShapeDtypeStruct((rows, width), BF16),
        cost_estimate=pl.CostEstimate(
            flops=4 * rows * features * width,
            bytes_accessed=2 * (2 * features * width + rows * (2 * features + width)),
            transcendentals=0,
        ),
    )(block.astype(jnp.int32).reshape(1), attended, retrieved, out_weight, cross_weight)


def project_and_sum(attended, retrieved, out_weight, cross_weight):
    groups = lax.axis_size("mp")
    own = lax.axis_index("mp")
    share = out_weight.shape[1] // groups
    core, chip = own % 2, own // 2
    came = []
    for step in range(groups // 2 - 1, -1, -1):
        pair = 2 * (chip ^ step)
        given = project(attended, retrieved, out_weight, cross_weight, pair + 1 - core, share)
        got = lax.ppermute(given, "mp", [(i, i ^ 1) for i in range(groups)])
        kept = project(attended, retrieved, out_weight, cross_weight, pair + core, share)
        total = kept.astype(F32) + got.astype(F32)
        if step:
            total, attended = lax.optimization_barrier((total.astype(BF16), attended))
            came.append(
                lax.ppermute(total, "mp", [(i, i ^ (2 * step)) for i in range(groups)])
            )
    for other in came:
        total = total + other.astype(F32)
    return total.astype(BF16)


def per_device(
    queries,
    self_keys,
    self_values,
    cross_query,
    memory_keys,
    memory_values,
    neighbour_owner,
    neighbour_slot,
    out_weight,
    cross_weight,
):
    devices = lax.axis_size("seq")
    rows, features = queries.shape
    heads = features // HEAD
    span_count, picks = neighbour_owner.shape
    requests = span_count * picks
    capacity = max(2, (requests + devices - 1) // devices)

    owners = neighbour_owner.reshape(requests)
    slots = neighbour_slot.reshape(requests)
    order = jnp.arange(requests, dtype=jnp.int32)
    ranks = jnp.sum(
        ((owners[:, None] == owners[None, :]) & (order[None, :] < order[:, None])).astype(
            jnp.int32
        ),
        axis=1,
    )
    target = owners * capacity + ranks
    hits = target[None, :] == jnp.arange(devices * capacity, dtype=jnp.int32)[:, None]
    indices = jnp.sum(jnp.where(hits, order[None, :] // picks, 0), axis=1)
    sent_slots = jnp.sum(jnp.where(hits, slots[None, :], 0), axis=1)

    asked = exchange(ask(cross_query, indices, sent_slots, devices, capacity))
    packed = pack_heads(queries, self_keys, self_values, devices)
    asked, packed = lax.optimization_barrier((asked, packed))
    data = exchange(packed)
    wanted = asked[:, capacity * SPAN, :capacity].astype(jnp.int32).reshape(devices * capacity)
    answered = answer(asked, wanted, memory_keys, memory_values, capacity)
    data, answered = lax.optimization_barrier((data, answered))
    answers = exchange(answered)
    attended = attend(data, rows)
    answers, attended = lax.optimization_barrier((answers, attended))
    attended = exchange(attended)
    retrieved = combine(answers, owners, ranks, span_count, picks, capacity)
    piece = attended.shape[1]
    attended = jnp.transpose(
        attended.reshape(heads, rows // piece, piece, HEAD), (1, 2, 0, 3)
    ).reshape(rows, features)
    return project_and_sum(attended, retrieved, out_weight, cross_weight)


def solution(mesh):
    placed = (
        P("seq", "mp"),
        P("seq", "mp"),
        P("seq", "mp"),
        P("seq", "mp"),
        P("seq", None, "mp"),
        P("seq", None, "mp"),
        P("seq", None),
        P("seq", None),
        P("mp", None),
        P("mp", None),
    )
    return jax.shard_map(
        per_device, mesh=mesh, in_specs=placed, out_specs=P("seq", "mp"), check_vma=False
    )
```

```python
import functools
import math

import jax
import jax.numpy as jnp
from jax import lax
from jax.experimental import pallas as pl
from jax.experimental.pallas import tpu as pltpu
from jax.sharding import PartitionSpec as P

HEAD = 128
SPAN = 64
NEG_FILL = -1e30
SCALE = HEAD ** (-0.5)
LOG2E = math.log2(math.e)
INFO = 16
F32 = jnp.float32
BF16 = jnp.bfloat16


def pack_heads_kernel(q_ref, k_ref, v_ref, out_ref):
    piece = q_ref.shape[0]
    rows = k_ref.shape[0]
    out_ref[0, :piece] = q_ref[...]
    out_ref[0, piece : piece + rows] = k_ref[...]
    out_ref[0, piece + rows :] = v_ref[...]


def pack_heads(queries, self_keys, self_values, devices):
    rows, features = queries.shape
    repeats = devices // (features // HEAD)
    piece = rows // repeats
    whole = pl.BlockSpec((rows, HEAD), lambda d: (0, d // repeats))
    return pl.pallas_call(
        pack_heads_kernel,
        grid=(devices,),
        out_shape=jax.ShapeDtypeStruct((devices, piece + 2 * rows, HEAD), BF16),
        in_specs=[
            pl.BlockSpec((piece, HEAD), lambda d: (d % repeats, d // repeats)),
            whole,
            whole,
        ],
        out_specs=pl.BlockSpec((1, piece + 2 * rows, HEAD), lambda d: (d, 0, 0)),
    )(queries, self_keys, self_values)


def attend_kernel(rows, rep_ref, data_ref, out_ref):
    source = pl.program_id(0)
    piece = out_ref.shape[1]
    query = data_ref[source, :piece]

    def scores_of(j):
        keys = data_ref[j, piece : piece + rows]
        return lax.dot_general(
            query, keys, (((1,), (1,)), ((), ())), preferred_element_type=F32
        ) * (SCALE * LOG2E)

    def mix(j, weights):
        return jnp.dot(
            weights.astype(BF16), data_ref[j, piece + rows :], preferred_element_type=F32
        )

    first = rep_ref[0] * piece
    row_ids = first + lax.broadcasted_iota(jnp.int32, (piece, rows), 0)
    col_ids = lax.broadcasted_iota(jnp.int32, (piece, rows), 1)
    scores = jnp.where(row_ids >= col_ids, scores_of(source), NEG_FILL)
    top = jnp.max(scores, axis=1, keepdims=True)
    weights = jnp.exp2(scores - top)
    total = jnp.sum(weights, axis=1, keepdims=True)
    acc = mix(source, weights)

    def body(j, state):
        top, total, acc = state
        scores = scores_of(j)
        newest = jnp.maximum(top, jnp.max(scores, axis=1, keepdims=True))
        weights = jnp.exp2(scores - newest)
        factor = jnp.exp2(top - newest)
        total = total * factor + jnp.sum(weights, axis=1, keepdims=True)
        return newest, total, acc * factor + mix(j, weights)

    top, total, acc = lax.fori_loop(0, source, body, (top, total, acc))
    out_ref[0] = (acc / total).astype(BF16)


def attend(data, rows):
    devices, height, _ = data.shape
    piece = height - 2 * rows
    heads = devices * piece // rows
    rep = (lax.axis_index("seq") % (rows // piece)).astype(jnp.int32).reshape(1)
    del heads
    return pl.pallas_call(
        functools.partial(attend_kernel, rows),
        grid_spec=pltpu.PrefetchScalarGridSpec(
            num_scalar_prefetch=1,
            grid=(devices,),
            in_specs=[pl.BlockSpec((devices, height, HEAD), lambda s, r: (0, 0, 0))],
            out_specs=pl.BlockSpec((1, piece, HEAD), lambda s, r: (s, 0, 0)),
        ),
        out_shape=jax.ShapeDtypeStruct((devices, piece, HEAD), BF16),
        compiler_params=pltpu.CompilerParams(vmem_limit_bytes=48 * 2**20),
    )(rep, data)


def ask_kernel(capacity, idx_ref, slot_ref, query_ref, out_ref):
    lanes = lax.broadcasted_iota(jnp.int32, (INFO, out_ref.shape[2]), 1)

    def body(dest, carry):
        info = jnp.zeros(lanes.shape, jnp.int32)
        for item in range(capacity):
            start = pl.multiple_of(idx_ref[dest * capacity + item] * SPAN, SPAN)
            out_ref[dest, item * SPAN : (item + 1) * SPAN] = query_ref[pl.ds(start, SPAN)]
            info = jnp.where(lanes == item, slot_ref[dest * capacity + item], info)
        out_ref[dest, capacity * SPAN :] = info.astype(F32).astype(BF16)
        return carry

    lax.fori_loop(0, out_ref.shape[0], body, 0)


def ask(cross_query, indices, slots, devices, capacity):
    features = cross_query.shape[1]
    height = capacity * SPAN + INFO
    return pl.pallas_call(
        functools.partial(ask_kernel, capacity),
        grid_spec=pltpu.PrefetchScalarGridSpec(
            num_scalar_prefetch=2,
            grid=(1,),
            in_specs=[pl.BlockSpec(cross_query.shape, lambda d, i, s: (0, 0))],
            out_specs=pl.BlockSpec((devices, height, features), lambda d, i, s: (0, 0, 0)),
        ),
        out_shape=jax.ShapeDtypeStruct((devices, height, features), BF16),
        compiler_params=pltpu.CompilerParams(vmem_limit_bytes=32 * 2**20),
    )(indices, slots, cross_query)


def answer_kernel(capacity, want_ref, asked_ref, *refs):
    out_ref = refs[-1]
    features = out_ref.shape[2]
    heads = features // HEAD
    lanes = lax.broadcasted_iota(jnp.int32, (SPAN, HEAD), 1)
    logs = []
    for item in range(capacity):
        keys_ref, values_ref = refs[item], refs[capacity + item]
        rows = slice(item * SPAN, (item + 1) * SPAN)
        info = jnp.zeros((SPAN, HEAD), F32)
        for head in range(heads):
            cols = slice(head * HEAD, (head + 1) * HEAD)
            scores = (
                lax.dot_general(
                    asked_ref[0, rows, cols],
                    keys_ref[0, :, cols],
                    (((1,), (1,)), ((), ())),
                    preferred_element_type=F32,
                )
                * SCALE
            )
            top = jnp.max(scores, axis=1, keepdims=True)
            weights = jnp.exp(scores - top)
            mass = jnp.sum(weights, axis=1, keepdims=True)
            blended = jnp.dot(
                weights.astype(BF16), values_ref[0, :, cols], preferred_element_type=F32
            )
            out_ref[0, rows, cols] = (blended / mass).astype(BF16)
            log_mass = top + jnp.log(mass)
            coarse = log_mass.astype(BF16).astype(F32)
            info = jnp.where(lanes == head, coarse, info)
            info = jnp.where(lanes == heads + head, log_mass - coarse, info)
        logs.append(info)
    turned = jnp.transpose(jnp.concatenate(logs, axis=0))
    out_ref[0, capacity * SPAN :] = jnp.zeros((INFO, features), BF16)
    out_ref[0, capacity * SPAN :, : capacity * SPAN] = turned[:INFO].astype(BF16)


def answer(asked, wanted, memory_keys, memory_values, capacity):
    devices, height, features = asked.shape
    length = memory_keys.shape[1]
    tiles = [
        pl.BlockSpec(
            (1, length, features), lambda s, w, item=item: (w[s * capacity + item], 0, 0)
        )
        for item in range(capacity)
    ]
    block = pl.BlockSpec((1, height, features), lambda s, w: (s, 0, 0))
    return pl.pallas_call(
        functools.partial(answer_kernel, capacity),
        grid_spec=pltpu.PrefetchScalarGridSpec(
            num_scalar_prefetch=1,
            grid=(devices,),
            in_specs=[block] + tiles + tiles,
            out_specs=block,
        ),
        out_shape=jax.ShapeDtypeStruct((devices, height, features), BF16),
    )(wanted, asked, *([memory_keys] * capacity), *([memory_values] * capacity))


def combine_kernel(picks, capacity, owner_ref, rank_ref, *refs):
    out_ref = refs[-1]
    span = pl.program_id(0)
    features = out_ref.shape[1]
    heads = features // HEAD
    starts, logs = [], []
    for n in range(picks):
        rank = rank_ref[span * picks + n]
        starts.append(pl.multiple_of(rank * SPAN, SPAN))
        info = refs[n][0, capacity * SPAN :, : capacity * SPAN].astype(F32)
        turned = jnp.transpose(info)
        chosen = turned[:SPAN]
        for item in range(1, capacity):
            chosen = jnp.where(rank == item, turned[item * SPAN : (item + 1) * SPAN], chosen)
        logs.append(chosen)
    for head in range(heads):
        cols = slice(head * HEAD, (head + 1) * HEAD)
        masses = [c[:, head : head + 1] + c[:, heads + head : heads + head + 1] for c in logs]
        best = functools.reduce(jnp.maximum, masses)
        shares = [jnp.exp(m - best) for m in masses]
        whole = sum(shares)
        mixed = sum(
            share * refs[n][0, pl.ds(starts[n], SPAN), cols].astype(F32)
            for n, share in enumerate(shares)
        )
        out_ref[:, cols] = (mixed / whole).astype(BF16)


def combine(answers, owners, ranks, span_count, picks, capacity):
    devices, height, features = answers.shape
    return pl.pallas_call(
        functools.partial(combine_kernel, picks, capacity),
        grid_spec=pltpu.PrefetchScalarGridSpec(
            num_scalar_prefetch=2,
            grid=(span_count,),
            in_specs=[
                pl.BlockSpec(
                    (1, height, features), lambda c, o, r, n=n: (o[c * picks + n], 0, 0)
                )
                for n in range(picks)
            ],
            out_specs=pl.BlockSpec((SPAN, features), lambda c, o, r: (c, 0)),
        ),
        out_shape=jax.ShapeDtypeStruct((span_count * SPAN, features), BF16),
    )(owners, ranks, *([answers] * picks))


def exchange(value):
    return lax.all_to_all(value, "seq", split_axis=0, concat_axis=0, tiled=True)


def project_kernel(block_ref, att_ref, ret_ref, out_weight_ref, cross_weight_ref, out_ref):
    total = jnp.dot(att_ref[...], out_weight_ref[...], preferred_element_type=F32)
    total += jnp.dot(ret_ref[...], cross_weight_ref[...], preferred_element_type=F32)
    out_ref[...] = total.astype(BF16)


def project(attended, retrieved, out_weight, cross_weight, block, width):
    rows, features = attended.shape
    tiles = 4
    tile = width // tiles
    left = pl.BlockSpec((rows, features), lambda t, b: (0, 0))
    right = pl.BlockSpec((features, tile), lambda t, b: (0, b[0] * tiles + t))
    return pl.pallas_call(
        project_kernel,
        grid_spec=pltpu.PrefetchScalarGridSpec(
            num_scalar_prefetch=1,
            grid=(tiles,),
            in_specs=[left, left, right, right],
            out_specs=pl.BlockSpec((rows, tile), lambda t, b: (0, t)),
        ),
        out_shape=jax.ShapeDtypeStruct((rows, width), BF16),
        cost_estimate=pl.CostEstimate(
            flops=4 * rows * features * width,
            bytes_accessed=2 * (2 * features * width + rows * (2 * features + width)),
            transcendentals=0,
        ),
    )(block.astype(jnp.int32).reshape(1), attended, retrieved, out_weight, cross_weight)


def project_and_sum(attended, retrieved, out_weight, cross_weight):
    groups = lax.axis_size("mp")
    own = lax.axis_index("mp")
    share = out_weight.shape[1] // groups
    core, chip = own % 2, own // 2
    came = []
    for step in range(groups // 2 - 1, -1, -1):
        pair = 2 * (chip ^ step)
        given = project(attended, retrieved, out_weight, cross_weight, pair + 1 - core, share)
        got = lax.ppermute(given, "mp", [(i, i ^ 1) for i in range(groups)])
        kept = project(attended, retrieved, out_weight, cross_weight, pair + core, share)
        total = kept.astype(F32) + got.astype(F32)
        if step:
            total, attended = lax.optimization_barrier((total.astype(BF16), attended))
            came.append(
                lax.ppermute(total, "mp", [(i, i ^ (2 * step)) for i in range(groups)])
            )
    for other in came:
        total = total + other.astype(F32)
    return total.astype(BF16)


def per_device(
    queries,
    self_keys,
    self_values,
    cross_query,
    memory_keys,
    memory_values,
    neighbour_owner,
    neighbour_slot,
    out_weight,
    cross_weight,
):
    devices = lax.axis_size("seq")
    rows, features = queries.shape
    heads = features // HEAD
    span_count, picks = neighbour_owner.shape
    requests = span_count * picks
    capacity = max(2, (requests + devices - 1) // devices)

    owners = neighbour_owner.reshape(requests)
    slots = neighbour_slot.reshape(requests)
    order = jnp.arange(requests, dtype=jnp.int32)
    ranks = jnp.sum(
        ((owners[:, None] == owners[None, :]) & (order[None, :] < order[:, None])).astype(
            jnp.int32
        ),
        axis=1,
    )
    target = owners * capacity + ranks
    hits = target[None, :] == jnp.arange(devices * capacity, dtype=jnp.int32)[:, None]
    indices = jnp.sum(jnp.where(hits, order[None, :] // picks, 0), axis=1)
    sent_slots = jnp.sum(jnp.where(hits, slots[None, :], 0), axis=1)

    asked = exchange(ask(cross_query, indices, sent_slots, devices, capacity))
    packed = pack_heads(queries, self_keys, self_values, devices)
    asked, packed = lax.optimization_barrier((asked, packed))
    data = exchange(packed)
    wanted = asked[:, capacity * SPAN, :capacity].astype(jnp.int32).reshape(devices * capacity)
    answered = answer(asked, wanted, memory_keys, memory_values, capacity)
    data, answered = lax.optimization_barrier((data, answered))
    answers = exchange(answered)
    attended = attend(data, rows)
    answers, attended = lax.optimization_barrier((answers, attended))
    attended = exchange(attended)
    retrieved = combine(answers, owners, ranks, span_count, picks, capacity)
    piece = attended.shape[1]
    attended = jnp.transpose(
        attended.reshape(heads, rows // piece, piece, HEAD), (1, 2, 0, 3)
    ).reshape(rows, features)
    return project_and_sum(attended, retrieved, out_weight, cross_weight)


def solution(mesh):
    placed = (
        P("seq", "mp"),
        P("seq", "mp"),
        P("seq", "mp"),
        P("seq", "mp"),
        P("seq", None, "mp"),
        P("seq", None, "mp"),
        P("seq", None),
        P("seq", None),
        P("mp", None),
        P("mp", None),
    )
    return jax.shard_map(
        per_device, mesh=mesh, in_specs=placed, out_specs=P("seq", "mp"), check_vma=False
    )
```
